512 devices in a mesh: expert: 8 (over x, z_hi), dp: 64 (over y, z_lo, core).
Axes of the slice: x: 4, y: 8, z: 8 (z_hi: 2, z_lo: 4; z = z_hi * 4 + z_lo), core: 2. Of those that a mesh axis runs over, the one named last changes fastest.
Arguments:
- output_gradient: bfloat16 [2048, 6144], P(('expert', 'dp')), may hold values from -6 to 6
- gates: float32 [2048, 2], P(('expert', 'dp')), may hold values from 0.2 to 1
- expert_index: int32 [2048, 2], P(('expert', 'dp')), may hold values from 0 to 7, all different within a row; in each aligned block of 4 rows (0 to 3, 4 to 7, ...) at most 2 rows name the same one
- hidden_state: bfloat16 [8, 1024, 16384], P('expert', None, 'dp'), may hold values from -6 to 6
- down_matrix: bfloat16 [8, 16384, 6144], P('expert', 'dp'), may hold values from -0.078125 to 0.078125
- left_adapter: bfloat16 [8, 16384, 16], P('expert', 'dp'), may hold values from -0.046875 to 0.046875
- right_adapter: bfloat16 [8, 16, 6144], P('expert'), may hold values from -0.078125 to 0.078125
Outputs:
- hidden_gradient: bfloat16 [8, 1024, 16384], P('expert', None, 'dp')
- left_gradient: float32 [8, 16384, 16], P('expert', 'dp')
- right_gradient: float32 [8, 16, 6144], P('expert')
The draws below stay inside these ranges and needn't reach their ends.
Inputs may be any that keep to these rules, and one draw needn't show every extreme that they name: `expert_index`: each token names 2 different experts; the tokens of one device name one expert at most 2 times.
All inputs are finite; a program needn't handle non-finite values.
Results may differ from the reference program's by a relative error of at most 0.0049.
Values may be sent and summed in bfloat16 or wider, within the bound.
A program may use at most 128 MiB of HBM per device.

```python
import math
import jax
import jax.numpy as jnp
import numpy as np
from jax import lax

MODEL_WIDTH = 6144
HIDDEN_UNITS = 16384
ADAPTER_RANK = 16
TOP = 2
TOK_DEV = 4
EXPERT_TOTAL = 8
CAP = 2
TOKENS = 2048
ROWS = 1024
N_EXPERT = 8
N_DP = 64


def steps_of(own_key, shape, shards, least, top_value):
    level, own = 1.0, jax.random.fold_in(own_key, 6)
    for dim, parts in shards:
        heights = jnp.exp(jax.random.uniform(jax.random.fold_in(own, dim), (parts,), jnp.float32, least / len(shards), top_value / len(shards)))
        level = level * jnp.repeat(heights, shape[dim] // parts).reshape([-1 if axis == dim else 1 for axis in range(len(shape))])
    return level


def shared_out(rng, own, number, rows, amount, top, most, skew):
    sequence = jax.random.permutation(rng, amount)
    packed, common = load_shares(amount, rows * top, most, skew, True), load_shares(amount, rows * top, most, skew, False)
    places = jnp.arange(amount)

    def named(tallies, rotation):
        used = int((tallies > 0).sum())
        fixed = max(1, used // 4)
        passed = fixed + (places - fixed + rotation * (used - fixed)) % max(1, amount - fixed)
        return jnp.zeros((amount,), jnp.int32).at[sequence[jnp.where(places < fixed, places, passed)]].set(jnp.asarray(tallies, jnp.int32))

    tallies = jnp.where(number % 4 == 0, named(packed, number // 4), named(common, number - number // 4 - 1))
    mixed = jax.random.permutation(jax.random.fold_in(own, 3), amount)
    source_of, taker = mixed[0:amount // 2 * 2:2], mixed[1:amount // 2 * 2:2]
    room = jnp.minimum(tallies[source_of] - 1, most - tallies[taker]) // 2
    room = jnp.where((source_of == sequence[0]) | (taker == sequence[0]) | (tallies[taker] == 0), 0, jnp.maximum(room, 0))
    passed = jax.random.randint(jax.random.fold_in(own, 4), (amount // 2,), 0, 1 << 20) % (room + 1)
    tallies = tallies.at[source_of].add(-passed).at[taker].add(passed)
    items = jnp.searchsorted(jnp.cumsum(tallies), jnp.arange(rows * top), side="right").astype(jnp.int32)
    grid = items.reshape(top, rows).T
    grid = grid[jax.random.permutation(jax.random.fold_in(own, 1), rows)]
    rotation = jax.random.randint(jax.random.fold_in(own, 2), (rows, 1), 0, top)
    return jnp.take_along_axis(grid, (jnp.arange(top)[None, :] + rotation) % top, axis=1)


def load_shares(count, total, limit, skew, full):
    weights = [(1 << 20) // math.isqrt(grade ** skew) + 1 for grade in range(1, count + 1)]
    largest = limit if full else min(limit, max(-(-total // count), total * weights[0] // sum(weights)))
    least = 1 if total - largest >= count - 1 else 0
    counts, rest = [largest] + [least] * (count - 1), total - largest - least * (count - 1)
    while rest > 0:
        movable = [i for i in range(1, count) if counts[i] < largest] or [i for i in range(1, count) if counts[i] < limit]
        pool, left = sum([weights[i] for i in movable]), rest
        for i in movable:
            addition = min(limit - counts[i], max(1, left * weights[i] // pool), rest)
            counts[i] = counts[i] + addition
            rest = rest - addition
    return np.array(counts)


def normal_values(rng, extent, spread, reach, cuts=(), held_as=jnp.bfloat16):
    values = spread * jax.random.normal(rng, extent, jnp.float32)
    if cuts:
        values = values * steps_of(rng, extent, cuts, -0.22, 0.18)
    return jnp.clip(values, -reach, reach).astype(held_as)


def setup_inputs(seed: int = 0) -> dict:
    key_list = jax.random.split(jax.random.key(seed), 8)
    output_gradient = normal_values(key_list[0], (TOKENS, MODEL_WIDTH), 1.0, 6.0, ((0, 512),))
    gates = jnp.clip(0.2 + 0.8 * jax.random.uniform(key_list[1], (TOKENS, TOP), jnp.float32) ** steps_of(key_list[1], (TOKENS, TOP), ((0, 512),), -0.2, 0.2), 0.2, 1.0)
    expert_index_keys = jax.random.split(jax.random.fold_in(key_list[2], 1), TOKENS // TOK_DEV)
    expert_index_turns = jax.random.permutation(jax.random.fold_in(key_list[2], 3), TOKENS // TOK_DEV)
    expert_index = jax.vmap(lambda own, number: shared_out(jax.random.fold_in(key_list[2], 2), own, number, TOK_DEV, EXPERT_TOTAL, TOP, CAP, 2))(expert_index_keys, expert_index_turns).reshape((TOKENS, TOP))
    hidden_state = normal_values(key_list[3], (EXPERT_TOTAL, ROWS, HIDDEN_UNITS), 1.0, 6.0, ((0, 8), (2, 64)))
    down_matrix = normal_values(key_list[4], (EXPERT_TOTAL, HIDDEN_UNITS, MODEL_WIDTH), MODEL_WIDTH ** -0.5, 0.078125, ((0, 8), (1, 64)))
    left_adapter = normal_values(key_list[5], (EXPERT_TOTAL, HIDDEN_UNITS, ADAPTER_RANK), HIDDEN_UNITS ** -0.5, 0.046875, ((0, 8), (1, 64)))
    right_adapter = normal_values(key_list[6], (EXPERT_TOTAL, ADAPTER_RANK, MODEL_WIDTH), MODEL_WIDTH ** -0.5, 0.078125, ((0, 8),))
    return dict(output_gradient=output_gradient, gates=gates, expert_index=expert_index, hidden_state=hidden_state, down_matrix=down_matrix, left_adapter=left_adapter, right_adapter=right_adapter)


adapter_scale = 2.0


def single_expert(inputs):
    token_rows, gated_input, weight, left_factor, right_factor = inputs
    reduced_rows = jnp.dot(token_rows, right_factor.T, preferred_element_type=jnp.float32).astype(jnp.bfloat16)
    frozen_path = jnp.dot(token_rows, weight.T, preferred_element_type=jnp.float32)
    adapter_delta = jnp.dot(reduced_rows, left_factor.T, preferred_element_type=jnp.float32)
    hidden_gradient = (frozen_path + adapter_scale * adapter_delta).astype(jnp.bfloat16)
    left_gradient = adapter_scale * jnp.dot(gated_input.T, reduced_rows, preferred_element_type=jnp.float32)
    adapter_factor = jnp.dot(gated_input, left_factor, preferred_element_type=jnp.float32).astype(jnp.bfloat16)
    right_gradient = adapter_scale * jnp.dot(adapter_factor.T, token_rows, preferred_element_type=jnp.float32)
    return hidden_gradient, left_gradient, right_gradient


def reference(output_gradient, gates, expert_index, hidden_state, down_matrix, left_adapter, right_adapter):
    scaled = (gates[:, :, None] * output_gradient[:, None, :].astype(jnp.float32)).astype(jnp.bfloat16)
    blocks = N_EXPERT * N_DP
    chosen = expert_index.reshape(blocks, TOK_DEV * TOP)
    onehot = (chosen[:, :, None] == jnp.arange(EXPERT_TOTAL, dtype=jnp.int32)[None, None, :]).astype(jnp.int32)
    before = jnp.cumsum(onehot, axis=1) - onehot
    position = jnp.sum(before * onehot, axis=2)
    group = jnp.arange(blocks, dtype=jnp.int32)[:, None]
    slot_row = (group % N_DP) * (N_EXPERT * CAP) + (group // N_DP) * CAP + position
    routed_rows = jnp.zeros((EXPERT_TOTAL, ROWS, MODEL_WIDTH), jnp.bfloat16)
    routed_rows = routed_rows.at[chosen.reshape(-1), slot_row.reshape(-1).astype(jnp.int32)].set(scaled.reshape(-1, MODEL_WIDTH))
    hidden_gradient, left_gradient, right_gradient = lax.map(single_expert, (routed_rows, hidden_state, down_matrix, left_adapter, right_adapter))
    return hidden_gradient, left_gradient, right_gradient
```

```python
import functools

import jax
import jax.numpy as jnp
from jax import lax
from jax.experimental import pallas as pl
from jax.experimental.pallas import tpu as pltpu
from jax.sharding import PartitionSpec as P

MESH = pl.DeviceIdType.MESH
F32, BF16 = jnp.float32, jnp.bfloat16
NT = (((1,), (1,)), ((), ()))
TN = (((0,), (0,)), ((), ()))

SIZES = dict(ring=8, run=4, across=1536, chunk=1024, limit=60 * 2**20)


def kernel(
    ring, run, across, chunk,
    grad_ref, gates_ref, index_ref, state_hbm, down_hbm, left_ref, right_ref,
    hidden_hbm, left_out, right_out,
    slots, mixed, rows, down, state, hidden, right_part,
    fact_send, fact_one, fact_two_send, fact_two, fact_three_send, fact_three,
    load_sem, store_sem, own_sem, mix_send, mix_recv,
    far_recv, near_recv, far_long, far_short, near_long, near_short, run_far, run_near,
    pair_send, pair_recv, f1s, f1r, f2s, f2r, f3s, f3r,
):
    width = grad_ref.shape[1]
    tokens, top = gates_ref.shape
    experts = slots.shape[0]
    cap = slots.shape[1]
    half = ring // 2
    group = run * 2
    block = experts * cap
    batch = group * block
    rank = left_ref.shape[2]
    along = width - across
    me = lax.axis_index("expert")
    v = lax.axis_index("dp")
    y, z, c = v // group, (v // 2) % run, v % 2
    sign = 1 - 2 * c

    def at(yy, zz, cc):
        return (me, (yy * run + zz) * 2 + cc)

    def wrap(value):
        return lax.rem(value + 2 * ring, ring)

    def peer(k):
        return lax.rem(z * 2 + c + k, group)

    load_down = pltpu.make_async_copy(down_hbm.at[0], down, load_sem.at[0])
    load_state = pltpu.make_async_copy(state_hbm.at[0], state, load_sem.at[1])
    load_state.start()
    load_down.start()

    barrier = pltpu.get_barrier_semaphore()
    for k in range(1, experts):
        pl.semaphore_signal(barrier, 1, device_id=(lax.rem(me + k, experts), v), device_id_type=MESH)
    for k in range(1, ring):
        pl.semaphore_signal(barrier, 1, device_id=at(wrap(y + k), z, c), device_id_type=MESH)
    for k in range(1, group):
        pl.semaphore_signal(barrier, 1, device_id=(me, y * group + peer(k)), device_id_type=MESH)

    chosen = [[index_ref[t, k] for k in range(top)] for t in range(tokens)]
    flat = [chosen[t][k] for t in range(tokens) for k in range(top)]
    place = lax.broadcasted_iota(jnp.int32, (block, 1), 0)
    total = jnp.zeros((block, width), F32)
    for t in range(tokens):
        weight = jnp.zeros((block, 1), F32)
        for k in range(top):
            position = jnp.int32(0)
            for earlier in flat[: t * top + k]:
                position = position + (earlier == chosen[t][k]).astype(jnp.int32)
            slot = chosen[t][k] * cap + position
            weight = weight + jnp.where(place == slot, gates_ref[t, k], jnp.float32(0))
        total = total + weight * grad_ref[pl.ds(t, 1), :].astype(F32)
    total = total.astype(BF16)
    for e in range(experts):
        slots[e] = total[e * cap:(e + 1) * cap, :]

    pl.semaphore_wait(barrier, experts + ring + group - 3)

    def mix(k):
        other = lax.rem(me + k, experts)
        return pltpu.make_async_remote_copy(
            src_ref=slots.at[other], dst_ref=mixed.at[me], send_sem=mix_send.at[k],
            recv_sem=mix_recv.at[k], device_id=(other, v), device_id_type=MESH)

    for k in range(1, experts):
        mix(k).start()
    own = pltpu.make_async_copy(slots.at[me], mixed.at[me], own_sem)
    own.start()

    load_state.wait()
    part = lax.dot_general(left_ref[0], state[...], (((0,), (1,)), ((), ())), preferred_element_type=F32)
    for i in range(ring):
        fact_send[i] = part[:, i * batch:(i + 1) * batch]

    def ring_copy(src, dst, send, recv, k, slot):
        return pltpu.make_async_remote_copy(
            src_ref=src, dst_ref=dst.at[slot], send_sem=send.at[k], recv_sem=recv.at[k],
            device_id=at(wrap(y + k), z, c), device_id_type=MESH)

    def f1(k):
        return ring_copy(fact_send.at[wrap(y + k)], fact_one, f1s, f1r, k, y)

    def f2(k):
        return pltpu.make_async_remote_copy(
            src_ref=fact_two_send, dst_ref=fact_two.at[z * 2 + c], send_sem=f2s.at[k], recv_sem=f2r.at[k],
            device_id=(me, y * group + peer(k)), device_id_type=MESH)

    def f3(k):
        return ring_copy(fact_three_send, fact_three, f3s, f3r, k, y)

    for k in range(1, ring):
        f1(k).start()
    fact_one[y] = fact_send[y]

    own.wait()
    for k in range(1, experts):
        mix(k).wait_recv()
    rows[y, z, c] = jnp.concatenate([mixed[e] for e in range(experts)], axis=0)

    def piece(yy, zz, far):
        return rows.at[yy, zz, c, :, pl.ds(0, along) if far else pl.ds(along, across)]

    def step(yy, zz, far, up, send, recv):
        ref = piece(yy, zz, far)
        return pltpu.make_async_remote_copy(
            src_ref=ref, dst_ref=ref, send_sem=send, recv_sem=recv,
            device_id=at(wrap(y + up), z, c), device_id_type=MESH)

    def far_step(hop, zz, long):
        up = sign if long else -sign
        yy = wrap(y - up * hop)
        send = (far_long if long else far_short).at[hop, zz]
        return step(yy, zz, True, up, send, far_recv.at[yy, zz])

    def near_step(hop, long):
        up = sign if long else -sign
        yy = wrap(y - up * hop)
        send = (near_long if long else near_short).at[hop]
        return step(yy, z, False, up, send, near_recv.at[yy, z])

    def far_arrive(hop, zz, long):
        up = sign if long else -sign
        yy = wrap(y - up * hop)
        step(yy, zz, True, up, far_long.at[0, 0], far_recv.at[yy, zz]).wait_recv()

    def near_arrive(hop, long):
        up = sign if long else -sign
        yy = wrap(y - up * hop)
        step(yy, z, False, up, near_long.at[0], near_recv.at[yy, z]).wait_recv()

    def run_step(yy, k, far):
        ref = piece(yy, z, far)
        return pltpu.make_async_remote_copy(
            src_ref=ref, dst_ref=ref, send_sem=run_far.at[k] if far else run_near.at[yy, k],
            recv_sem=(far_recv if far else near_recv).at[yy, z],
            device_id=at(y, lax.rem(z + k, run), c), device_id_type=MESH)

    def run_arrive(yy, k, far):
        zz = lax.rem(z + run - k, run)
        ref = piece(yy, zz, far)
        pltpu.make_async_remote_copy(
            src_ref=ref, dst_ref=ref, send_sem=run_far.at[k],
            recv_sem=(far_recv if far else near_recv).at[yy, zz],
            device_id=at(y, zz, c), device_id_type=MESH).wait_recv()

    def pair(yy, cc):
        ref = rows.at[yy, :, cc]
        return pltpu.make_async_remote_copy(
            src_ref=ref, dst_ref=ref, send_sem=pair_send.at[yy], recv_sem=pair_recv.at[yy],
            device_id=at(y, z, 1 - c), device_id_type=MESH)

    near_step(0, True).start()
    near_step(0, False).start()
    far_step(0, z, True).start()
    far_step(0, z, False).start()
    for k in range(1, run):
        run_step(y, k, True).start()
    for k in range(1, run):
        run_step(y, k, False).start()

    for k in range(1, ring):
        f1(k).wait_recv()
    fact_two_send[...] = functools.reduce(lambda a, b: a + b, [fact_one[i] for i in range(ring)])
    for k in range(1, group):
        f2(k).start()
    fact_two[z * 2 + c] = fact_two_send[...]

    def near_round(hop):
        near_arrive(hop, True)
        pl.when(hop < half)(lambda: near_step(hop, True).start())
        yy = wrap(y - sign * hop)
        for k in range(1, run):
            run_step(yy, k, False).start()

        @pl.when(hop < half)
        def _():
            near_arrive(hop, False)
            pl.when(hop < half - 1)(lambda: near_step(hop, False).start())
            back = wrap(y + sign * hop)
            for k in range(1, run):
                run_step(back, k, False).start()

    for k in range(1, run):
        run_arrive(y, k, True)
        zz = lax.rem(z + run - k, run)
        far_step(0, zz, True).start()
        far_step(0, zz, False).start()
        if k == 1:
            near_round(jnp.int32(1))
    for k in range(1, group):
        f2(k).wait_recv()
    fact_three_send[...] = functools.reduce(lambda a, b: a + b, [fact_two[i] for i in range(group)])
    for k in range(1, ring):
        f3(k).start()
    fact_three[y] = fact_three_send[...]

    for k in range(1, run):
        run_arrive(y, k, False)
    pair(y, c).start()

    load_down.wait()
    left_out[0] = jnp.zeros(left_out.shape[1:], F32)

    def store(yy):
        return pltpu.make_async_copy(
            hidden.at[yy], hidden_hbm.at[0, pl.ds(pl.multiple_of(yy * batch, batch), batch), :], store_sem.at[yy])

    def compute(yy):
        pair(yy, 1 - c).wait_recv()
        factor = fact_three[yy].astype(BF16)
        units = down.shape[0]

        def body(i, carry):
            wide, low = carry
            columns = pl.ds(pl.multiple_of(i * chunk, chunk), chunk)
            x = rows[yy, :, :, :, columns].reshape(batch, chunk)
            wide = wide + lax.dot_general(x, down[:, columns], NT, preferred_element_type=F32)
            low = low + lax.dot_general(x, right_ref[0, :, columns], NT, preferred_element_type=F32)
            right_part[yy, :, columns] = jnp.dot(factor, x, preferred_element_type=F32)
            return wide, low

        wide, low = lax.fori_loop(
            0, width // chunk, body, (jnp.zeros((batch, units), F32), jnp.zeros((batch, rank), F32)))
        low = low.astype(BF16)
        delta = lax.dot_general(low, left_ref[0], NT, preferred_element_type=F32)
        hidden[yy] = (wide + 2.0 * delta).astype(BF16)
        store(yy).start()
        mine = state[pl.ds(pl.multiple_of(yy * batch, batch), batch), :]
        left_out[0] += 2.0 * lax.dot_general(mine, low, TN, preferred_element_type=F32)

    def order(n):
        hop = (n + 1) // 2
        return wrap(y + jnp.where(n % 2 == 1, -sign, sign) * hop)

    per = run // 2

    def turn(t, _):
        hop = t // 2 + 1
        odd = t % 2

        @pl.when(t < 2 * half)
        def _():
            for i in range(per):
                zz = lax.rem(z + run - (odd * per + i), run)
                far_arrive(hop, zz, True)
                pl.when(hop < half)(lambda: far_step(hop, zz, True).start())

                @pl.when(hop < half)
                def _():
                    far_arrive(hop, zz, False)
                    pl.when(hop < half - 1)(lambda: far_step(hop, zz, False).start())

            @pl.when((odd == 0) & (hop < half))
            def _():
                near_round(hop + 1)

            @pl.when(odd == 1)
            def _():
                yy = wrap(y - sign * hop)
                for k in range(1, run):
                    run_arrive(yy, k, False)
                pair(yy, c).start()

                @pl.when(hop < half)
                def _():
                    back = wrap(y + sign * hop)
                    for k in range(1, run):
                        run_arrive(back, k, False)
                    pair(back, c).start()

            @pl.when(t == 0)
            def _():
                for k in range(1, ring):
                    f3(k).wait_recv()

        @pl.when(t >= 1)
        def _():
            compute(order(t - 1))

        return 0

    lax.fori_loop(0, 2 * half + 1, turn, 0)

    right_out[0] = 2.0 * functools.reduce(lambda a, b: a + b, [right_part[i] for i in range(ring)])

    for k in range(1, experts):
        mix(k).wait_send()
    for k in range(1, ring):
        f1(k).wait_send()
        f3(k).wait_send()
    for k in range(1, group):
        f2(k).wait_send()
    for k in range(1, run):
        run_step(y, k, True).wait_send()

    def drain(i, _):
        store(i).wait()
        pair(i, c).wait_send()
        for k in range(1, run):
            run_step(i, k, False).wait_send()
        return 0

    lax.fori_loop(0, ring, drain, 0)
    for hop in range(half):
        near_step(hop, True).wait_send()
        if hop < half - 1:
            near_step(hop, False).wait_send()
        for zz in range(run):
            far_step(hop, zz, True).wait_send()
            if hop < half - 1:
                far_step(hop, zz, False).wait_send()


def shards(ring, run, across, chunk, limit, grad, gates, index, state, down, left, right):
    experts = lax.axis_size("expert")
    width = grad.shape[1]
    slots, units = state.shape[1:]
    rank = right.shape[1]
    half, group = ring // 2, run * 2
    block = slots // (ring * group)
    cap = block // experts
    batch = group * block
    dma = pltpu.SemaphoreType.DMA
    vmem = pl.BlockSpec(memory_space=pltpu.VMEM)
    smem = pl.BlockSpec(memory_space=pltpu.SMEM)
    hbm = pl.BlockSpec(memory_space=pl.ANY)
    return pl.pallas_call(
        functools.partial(kernel, ring, run, across, chunk),
        out_shape=(
            jax.ShapeDtypeStruct((1, slots, units), BF16),
            jax.ShapeDtypeStruct((1, units, rank), F32),
            jax.ShapeDtypeStruct((1, rank, width), F32),
        ),
        in_specs=[vmem, smem, smem, hbm, hbm, vmem, vmem],
        out_specs=(hbm, vmem, vmem),
        scratch_shapes=[
            pltpu.VMEM((experts, cap, width), BF16),
            pltpu.VMEM((experts, cap, width), BF16),
            pltpu.VMEM((ring, run, 2, block, width), BF16),
            pltpu.VMEM((units, width), BF16),
            pltpu.VMEM((slots, units), BF16),
            pltpu.VMEM((ring, batch, units), BF16),
            pltpu.VMEM((ring, rank, width), F32),
            pltpu.VMEM((ring, rank, batch), F32),
            pltpu.VMEM((ring, rank, batch), F32),
            pltpu.VMEM((rank, batch), F32),
            pltpu.VMEM((group, rank, batch), F32),
            pltpu.VMEM((rank, batch), F32),
            pltpu.VMEM((ring, rank, batch), F32),
            dma((2,)), dma((ring,)), dma, dma((experts,)), dma((experts,)),
            dma((ring, run)), dma((ring, run)), dma((half, run)), dma((half, run)),
            dma((half,)), dma((half,)), dma((run,)), dma((ring, run)),
            dma((ring,)), dma((ring,)),
            dma((ring,)), dma((ring,)), dma((group,)), dma((group,)), dma((ring,)), dma((ring,)),
        ],
        compiler_params=pltpu.CompilerParams(
            collective_id=0, has_side_effects=True, vmem_limit_bytes=limit),
    )(grad, gates, index, state, down, left, right)


def solution(mesh, **sizes):
    in_specs = (
        P(("expert", "dp"), None),
        P(("expert", "dp"), None),
        P(("expert", "dp"), None),
        P("expert", None, "dp"),
        P("expert", "dp", None),
        P("expert", "dp", None),
        P("expert", None, None),
    )
    out_specs = (P("expert", None, "dp"), P("expert", "dp", None), P("expert", None, None))
    sizes = dict(SIZES, **sizes)
    body = functools.partial(
        shards, sizes["ring"], sizes["run"], sizes["across"], sizes["chunk"], sizes["limit"])
    return jax.shard_map(body, mesh=mesh, in_specs=in_specs, out_specs=out_specs, check_vma=False)
```

```python
import functools

import jax
import jax.numpy as jnp
from jax import lax
from jax.experimental import pallas as pl
from jax.experimental.pallas import tpu as pltpu
from jax.sharding import PartitionSpec as P

MESH = pl.DeviceIdType.MESH
F32, BF16 = jnp.float32, jnp.bfloat16
NT = (((1,), (1,)), ((), ()))
TN = (((0,), (0,)), ((), ()))

SIZES = dict(ring=8, run=4, across=1536, chunk=1024, limit=60 * 2**20)


def kernel(
    ring, run, across, chunk,
    grad_ref, gates_ref, index_ref, state_hbm, down_hbm, left_ref, right_ref,
    hidden_hbm, left_out, right_out,
    slots, mixed, rows, down, state, hidden, right_part,
    fact_send, fact_one, fact_two_send, fact_two, fact_three_send, fact_three,
    load_sem, store_sem, own_sem, mix_send, mix_recv,
    far_recv, near_recv, far_long, far_short, near_long, near_short, run_far, run_near,
    pair_send, pair_recv, f1s, f1r, f2s, f2r, f3s, f3r,
):
    width = grad_ref.shape[1]
    top, tokens = gates_ref.shape
    experts = slots.shape[0]
    cap = slots.shape[1]
    half = ring // 2
    group = run * 2
    block = experts * cap
    batch = group * block
    rank = left_ref.shape[1]
    along = width - across
    me = lax.axis_index("expert")
    v = lax.axis_index("dp")
    y, z, c = v // group, (v // 2) % run, v % 2
    sign = 1 - 2 * c

    def at(yy, zz, cc):
        return (me, (yy * run + zz) * 2 + cc)

    def wrap(value):
        return lax.rem(value + 2 * ring, ring)

    def peer(k):
        return lax.rem(z * 2 + c + k, group)

    load_down = pltpu.make_async_copy(down_hbm.at[0], down, load_sem.at[0])
    load_state = pltpu.make_async_copy(state_hbm.at[0], state, load_sem.at[1])
    load_state.start()
    load_down.start()

    barrier = pltpu.get_barrier_semaphore()
    for k in range(1, experts):
        pl.semaphore_signal(barrier, 1, device_id=(lax.rem(me + k, experts), v), device_id_type=MESH)
    for k in range(1, ring):
        pl.semaphore_signal(barrier, 1, device_id=at(wrap(y + k), z, c), device_id_type=MESH)
    for k in range(1, group):
        pl.semaphore_signal(barrier, 1, device_id=(me, y * group + peer(k)), device_id_type=MESH)

    chosen = [[index_ref[k, t] for k in range(top)] for t in range(tokens)]
    flat = [chosen[t][k] for t in range(tokens) for k in range(top)]
    place = lax.broadcasted_iota(jnp.int32, (block, 1), 0)
    total = jnp.zeros((block, width), F32)
    for t in range(tokens):
        weight = jnp.zeros((block, 1), F32)
        for k in range(top):
            position = jnp.int32(0)
            for earlier in flat[: t * top + k]:
                position = position + (earlier == chosen[t][k]).astype(jnp.int32)
            slot = chosen[t][k] * cap + position
            weight = weight + jnp.where(place == slot, gates_ref[k, t], jnp.float32(0))
        total = total + weight * grad_ref[pl.ds(t, 1), :].astype(F32)
    total = total.astype(BF16)
    for e in range(experts):
        slots[e] = total[e * cap:(e + 1) * cap, :]

    pl.semaphore_wait(barrier, experts + ring + group - 3)

    def mix(k):
        other = lax.rem(me + k, experts)
        return pltpu.make_async_remote_copy(
            src_ref=slots.at[other], dst_ref=mixed.at[me], send_sem=mix_send.at[k],
            recv_sem=mix_recv.at[k], device_id=(other, v), device_id_type=MESH)

    for k in range(1, experts):
        mix(k).start()
    own = pltpu.make_async_copy(slots.at[me], mixed.at[me], own_sem)
    own.start()

    load_state.wait()
    part = lax.dot_general(left_ref[0], state[...], NT, preferred_element_type=F32)
    for i in range(ring):
        fact_send[i] = part[:, i * batch:(i + 1) * batch]

    def ring_copy(src, dst, send, recv, k, slot):
        return pltpu.make_async_remote_copy(
            src_ref=src, dst_ref=dst.at[slot], send_sem=send.at[k], recv_sem=recv.at[k],
            device_id=at(wrap(y + k), z, c), device_id_type=MESH)

    def f1(k):
        return ring_copy(fact_send.at[wrap(y + k)], fact_one, f1s, f1r, k, y)

    def f2(k):
        return pltpu.make_async_remote_copy(
            src_ref=fact_two_send, dst_ref=fact_two.at[z * 2 + c], send_sem=f2s.at[k], recv_sem=f2r.at[k],
            device_id=(me, y * group + peer(k)), device_id_type=MESH)

    def f3(k):
        return ring_copy(fact_three_send, fact_three, f3s, f3r, k, y)

    for k in range(1, ring):
        f1(k).start()
    fact_one[y] = fact_send[y]

    own.wait()
    for k in range(1, experts):
        mix(k).wait_recv()
    rows[y, z, c] = jnp.concatenate([mixed[e] for e in range(experts)], axis=0)

    def piece(yy, zz, far):
        return rows.at[yy, zz, c, :, pl.ds(0, along) if far else pl.ds(along, across)]

    def step(yy, zz, far, up, send, recv):
        ref = piece(yy, zz, far)
        return pltpu.make_async_remote_copy(
            src_ref=ref, dst_ref=ref, send_sem=send, recv_sem=recv,
            device_id=at(wrap(y + up), z, c), device_id_type=MESH)

    def far_step(hop, zz, long):
        up = sign if long else -sign
        yy = wrap(y - up * hop)
        send = (far_long if long else far_short).at[hop, zz]
        return step(yy, zz, True, up, send, far_recv.at[yy, zz])

    def near_step(hop, long):
        up = sign if long else -sign
        yy = wrap(y - up * hop)
        send = (near_long if long else near_short).at[hop]
        return step(yy, z, False, up, send, near_recv.at[yy, z])

    def far_arrive(hop, zz, long):
        up = sign if long else -sign
        yy = wrap(y - up * hop)
        step(yy, zz, True, up, far_long.at[0, 0], far_recv.at[yy, zz]).wait_recv()

    def near_arrive(hop, long):
        up = sign if long else -sign
        yy = wrap(y - up * hop)
        step(yy, z, False, up, near_long.at[0], near_recv.at[yy, z]).wait_recv()

    def run_step(yy, k, far):
        ref = piece(yy, z, far)
        return pltpu.make_async_remote_copy(
            src_ref=ref, dst_ref=ref, send_sem=run_far.at[k] if far else run_near.at[yy, k],
            recv_sem=(far_recv if far else near_recv).at[yy, z],
            device_id=at(y, lax.rem(z + k, run), c), device_id_type=MESH)

    def run_arrive(yy, k, far):
        zz = lax.rem(z + run - k, run)
        ref = piece(yy, zz, far)
        pltpu.make_async_remote_copy(
            src_ref=ref, dst_ref=ref, send_sem=run_far.at[k],
            recv_sem=(far_recv if far else near_recv).at[yy, zz],
            device_id=at(y, zz, c), device_id_type=MESH).wait_recv()

    def pair(yy, cc):
        ref = rows.at[yy, :, cc]
        return pltpu.make_async_remote_copy(
            src_ref=ref, dst_ref=ref, send_sem=pair_send.at[yy], recv_sem=pair_recv.at[yy],
            device_id=at(y, z, 1 - c), device_id_type=MESH)

    near_step(0, True).start()
    near_step(0, False).start()
    far_step(0, z, True).start()
    far_step(0, z, False).start()
    for k in range(1, run):
        run_step(y, k, True).start()
    for k in range(1, run):
        run_step(y, k, False).start()

    for k in range(1, ring):
        f1(k).wait_recv()
    fact_two_send[...] = functools.reduce(lambda a, b: a + b, [fact_one[i] for i in range(ring)])
    for k in range(1, group):
        f2(k).start()
    fact_two[z * 2 + c] = fact_two_send[...]

    def near_turn(hop):
        near_arrive(hop, True)
        if hop < half:
            near_step(hop, True).start()
            near_arrive(hop, False)
            if hop < half - 1:
                near_step(hop, False).start()

    def near_out(hop):
        for k in range(1, run):
            run_step(wrap(y - sign * hop), k, False).start()
        if hop < half:
            for k in range(1, run):
                run_step(wrap(y + sign * hop), k, False).start()

    def far_turn(hop, zz):
        far_arrive(hop, zz, True)
        pl.when(hop < half)(lambda: far_step(hop, zz, True).start())

        @pl.when(hop < half)
        def _():
            far_arrive(hop, zz, False)
            pl.when(hop < half - 1)(lambda: far_step(hop, zz, False).start())

    for hop in range(1, half + 1):
        near_turn(hop)
        far_turn(jnp.int32(hop), z)
        if hop == half // 2:
            for k in range(1, run):
                run_arrive(y, k, True)
                zz = lax.rem(z + run - k, run)
                far_step(0, zz, True).start()
                far_step(0, zz, False).start()
            for k in range(1, group):
                f2(k).wait_recv()
            fact_three_send[...] = functools.reduce(lambda a, b: a + b, [fact_two[i] for i in range(group)])
            for k in range(1, ring):
                f3(k).start()
            fact_three[y] = fact_three_send[...]
            for earlier in range(1, hop):
                near_out(earlier)
        if hop >= half // 2:
            near_out(hop)

    for k in range(1, run):
        run_arrive(y, k, False)
    pair(y, c).start()

    load_down.wait()
    left_out[0] = jnp.zeros(left_out.shape[1:], F32)

    def store(yy):
        return pltpu.make_async_copy(
            hidden.at[yy], hidden_hbm.at[0, pl.ds(pl.multiple_of(yy * batch, batch), batch), :], store_sem.at[yy])

    def compute(yy):
        pair(yy, 1 - c).wait_recv()
        factor = fact_three[yy].astype(BF16)
        units = down.shape[0]

        def body(i, carry):
            wide, low = carry
            columns = pl.ds(pl.multiple_of(i * chunk, chunk), chunk)
            x = rows[yy, :, :, :, columns].reshape(batch, chunk)
            wide = wide + lax.dot_general(x, down[:, columns], NT, preferred_element_type=F32)
            low = low + lax.dot_general(x, right_ref[0, :, columns], NT, preferred_element_type=F32)
            right_part[yy, :, columns] = jnp.dot(factor, x, preferred_element_type=F32)
            return wide, low

        wide, low = lax.fori_loop(
            0, width // chunk, body, (jnp.zeros((batch, units), F32), jnp.zeros((batch, rank), F32)))
        low = low.astype(BF16)
        delta = jnp.dot(low, left_ref[0], preferred_element_type=F32)
        hidden[yy] = (wide + 2.0 * delta).astype(BF16)
        store(yy).start()
        mine = state[pl.ds(pl.multiple_of(yy * batch, batch), batch), :]
        left_out[0] += 2.0 * lax.dot_general(low, mine, TN, preferred_element_type=F32)

    def order(n):
        hop = (n + 1) // 2
        return wrap(y + jnp.where(n % 2 == 1, -sign, sign) * hop)

    first = run // 2

    def turn(t, _):
        hop = t // 2 + 1

        @pl.when(t % 2 == 0)
        def _():
            for k in range(1, first):
                far_turn(hop, lax.rem(z + run - k, run))

        @pl.when(t % 2 == 1)
        def _():
            for k in range(first, run):
                far_turn(hop, lax.rem(z + run - k, run))
            yy = wrap(y - sign * hop)
            for k in range(1, run):
                run_arrive(yy, k, False)
            pair(yy, c).start()

            @pl.when(hop < half)
            def _():
                back = wrap(y + sign * hop)
                for k in range(1, run):
                    run_arrive(back, k, False)
                pair(back, c).start()

        @pl.when(t == 0)
        def _():
            for k in range(1, ring):
                f3(k).wait_recv()

        def one(n, _):
            compute(order(n))
            return 0

        start = jnp.where(t < 2 * half - 1, jnp.maximum(t - 1, 0), ring - 1)
        lax.fori_loop(start, jnp.where(t < 2 * half - 2, t, ring - 1), one, 0)
        return 0

    lax.fori_loop(0, 2 * half, turn, 0)
    compute(order(ring - 1))

    right_out[0] = 2.0 * functools.reduce(lambda a, b: a + b, [right_part[i] for i in range(ring)])

    for k in range(1, experts):
        mix(k).wait_send()
    for k in range(1, ring):
        f1(k).wait_send()
        f3(k).wait_send()
    for k in range(1, group):
        f2(k).wait_send()
    for k in range(1, run):
        run_step(y, k, True).wait_send()

    def drain(i, _):
        store(i).wait()
        pair(i, c).wait_send()
        for k in range(1, run):
            run_step(i, k, False).wait_send()
        return 0

    lax.fori_loop(0, ring, drain, 0)
    for hop in range(half):
        near_step(hop, True).wait_send()
        if hop < half - 1:
            near_step(hop, False).wait_send()
        for zz in range(run):
            far_step(hop, zz, True).wait_send()
            if hop < half - 1:
                far_step(hop, zz, False).wait_send()


def finish(a, b, c, a_out, b_out, c_out, a_mid, b_mid, c_mid, load, store):
    parts = [(a, a_mid, a_out), (b, b_mid, b_out), (c, c_mid, c_out)]
    loads = [pltpu.make_async_copy(x, m, load.at[i]) for i, (x, m, o) in enumerate(parts)]
    stores = [pltpu.make_async_copy(m, o, store.at[i]) for i, (x, m, o) in enumerate(parts)]
    for copy in loads:
        copy.start()
    for copy, after in zip(loads, stores):
        copy.wait()
        after.start()
    for copy in stores:
        copy.wait()


def shards(ring, run, across, chunk, limit, grad, gates, index, state, down, left, right):
    experts = lax.axis_size("expert")
    width = grad.shape[1]
    slots, units = state.shape[1:]
    rank = right.shape[1]
    half, group = ring // 2, run * 2
    block = slots // (ring * group)
    cap = block // experts
    batch = group * block
    dma = pltpu.SemaphoreType.DMA
    vmem = pl.BlockSpec(memory_space=pltpu.VMEM)
    smem = pl.BlockSpec(memory_space=pltpu.SMEM)
    hbm = pl.BlockSpec(memory_space=pl.ANY)
    results = pl.pallas_call(
        functools.partial(kernel, ring, run, across, chunk),
        out_shape=(
            jax.ShapeDtypeStruct((1, slots, units), BF16),
            jax.ShapeDtypeStruct((1, rank, units), F32),
            jax.ShapeDtypeStruct((1, rank, width), F32),
        ),
        in_specs=[vmem, smem, smem, hbm, hbm, vmem, vmem],
        out_specs=(hbm, vmem, vmem),
        scratch_shapes=[
            pltpu.VMEM((experts, cap, width), BF16),
            pltpu.VMEM((experts, cap, width), BF16),
            pltpu.VMEM((ring, run, 2, block, width), BF16),
            pltpu.VMEM((units, width), BF16),
            pltpu.VMEM((slots, units), BF16),
            pltpu.VMEM((ring, batch, units), BF16),
            pltpu.VMEM((ring, rank, width), F32),
            pltpu.VMEM((ring, rank, batch), F32),
            pltpu.VMEM((ring, rank, batch), F32),
            pltpu.VMEM((rank, batch), F32),
            pltpu.VMEM((group, rank, batch), F32),
            pltpu.VMEM((rank, batch), F32),
            pltpu.VMEM((ring, rank, batch), F32),
            dma((2,)), dma((ring,)), dma, dma((experts,)), dma((experts,)),
            dma((ring, run)), dma((ring, run)), dma((half, run)), dma((half, run)),
            dma((half,)), dma((half,)), dma((run,)), dma((ring, run)),
            dma((ring,)), dma((ring,)),
            dma((ring,)), dma((ring,)), dma((group,)), dma((group,)), dma((ring,)), dma((ring,)),
        ],
        compiler_params=pltpu.CompilerParams(
            collective_id=0, has_side_effects=True, vmem_limit_bytes=limit),
    )(grad, gates.T, index.T, state, down, jnp.swapaxes(left, 1, 2), right)
    hidden_gradient, left_gradient, right_gradient = pl.pallas_call(
        finish,
        out_shape=tuple(jax.ShapeDtypeStruct(r.shape, r.dtype) for r in results),
        in_specs=[hbm] * 3,
        out_specs=(hbm,) * 3,
        scratch_shapes=[pltpu.VMEM(r.shape, r.dtype) for r in results] + [dma((3,)), dma((3,))],
        compiler_params=pltpu.CompilerParams(vmem_limit_bytes=limit),
    )(*results)
    return hidden_gradient, jnp.swapaxes(left_gradient, 1, 2), right_gradient


def solution(mesh, **sizes):
    in_specs = (
        P(("expert", "dp"), None),
        P(("expert", "dp"), None),
        P(("expert", "dp"), None),
        P("expert", None, "dp"),
        P("expert", "dp", None),
        P("expert", "dp", None),
        P("expert", None, None),
    )
    out_specs = (P("expert", None, "dp"), P("expert", "dp", None), P("expert", None, None))
    sizes = dict(SIZES, **sizes)
    body = functools.partial(
        shards, sizes["ring"], sizes["run"], sizes["across"], sizes["chunk"], sizes["limit"])
    return jax.shard_map(body, mesh=mesh, in_specs=in_specs, out_specs=out_specs, check_vma=False)
```

```python
import functools

import jax
import jax.numpy as jnp
from jax import lax
from jax.experimental import pallas as pl
from jax.experimental.pallas import tpu as pltpu
from jax.sharding import PartitionSpec as P

MESH = pl.DeviceIdType.MESH
F32, BF16 = jnp.float32, jnp.bfloat16
NT = (((1,), (1,)), ((), ()))
TN = (((0,), (0,)), ((), ()))

SIZES = dict(ring=8, run=4, across=1536, chunk=3072, limit=60 * 2**20)


def kernel(
    ring, run, across, chunk,
    grad_ref, gates_ref, index_ref, state_hbm, down_hbm, left_ref, right_ref,
    hidden_hbm, left_out, right_out,
    slots, mixed, rows, down, state, hidden, right_part,
    fact_send, fact_one, fact_two_send, fact_two, fact_three_send, fact_three,
    load_sem, store_sem, own_sem, mix_send, mix_recv,
    far_recv, near_recv, far_long, far_short, near_long, near_short, run_far, run_near,
    pair_send, pair_recv, f1s, f1r, f2s, f2r, f3s, f3r,
):
    width = grad_ref.shape[1]
    top, tokens = gates_ref.shape
    experts = slots.shape[0]
    cap = slots.shape[1]
    half = ring // 2
    group = run * 2
    block = experts * cap
    batch = group * block
    rank = left_ref.shape[1]
    along = width - across
    me = lax.axis_index("expert")
    v = lax.axis_index("dp")
    y, z, c = v // group, (v // 2) % run, v % 2
    sign = 1 - 2 * c

    def at(yy, zz, cc):
        return (me, (yy * run + zz) * 2 + cc)

    def wrap(value):
        return lax.rem(value + 2 * ring, ring)

    def peer(k):
        return lax.rem(z * 2 + c + k, group)

    load_down = pltpu.make_async_copy(down_hbm.at[0], down, load_sem.at[0])
    load_state = pltpu.make_async_copy(state_hbm.at[0], state, load_sem.at[1])
    load_state.start()
    load_down.start()

    barrier = pltpu.get_barrier_semaphore()
    for k in range(1, experts):
        pl.semaphore_signal(barrier, 1, device_id=(lax.rem(me + k, experts), v), device_id_type=MESH)
    for k in range(1, ring):
        pl.semaphore_signal(barrier, 1, device_id=at(wrap(y + k), z, c), device_id_type=MESH)
    for k in range(1, group):
        pl.semaphore_signal(barrier, 1, device_id=(me, y * group + peer(k)), device_id_type=MESH)

    chosen = [[index_ref[k, t] for k in range(top)] for t in range(tokens)]
    flat = [chosen[t][k] for t in range(tokens) for k in range(top)]
    place = lax.broadcasted_iota(jnp.int32, (block, 1), 0)
    total = jnp.zeros((block, width), F32)
    for t in range(tokens):
        weight = jnp.zeros((block, 1), F32)
        for k in range(top):
            position = jnp.int32(0)
            for earlier in flat[: t * top + k]:
                position = position + (earlier == chosen[t][k]).astype(jnp.int32)
            slot = chosen[t][k] * cap + position
            weight = weight + jnp.where(place == slot, gates_ref[k, t], jnp.float32(0))
        total = total + weight * grad_ref[pl.ds(t, 1), :].astype(F32)
    total = total.astype(BF16)
    for e in range(experts):
        slots[e] = total[e * cap:(e + 1) * cap, :]

    pl.semaphore_wait(barrier, experts + ring + group - 3)

    def mix(k):
        other = lax.rem(me + k, experts)
        return pltpu.make_async_remote_copy(
            src_ref=slots.at[other], dst_ref=mixed.at[me], send_sem=mix_send.at[k],
            recv_sem=mix_recv.at[k], device_id=(other, v), device_id_type=MESH)

    for k in range(1, experts):
        mix(k).start()
    own = pltpu.make_async_copy(slots.at[me], mixed.at[me], own_sem)
    own.start()

    load_state.wait()
    part = lax.dot_general(left_ref[0], state[...], NT, preferred_element_type=F32)
    for i in range(ring):
        fact_send[i] = part[:, i * batch:(i + 1) * batch]

    def ring_copy(src, dst, send, recv, k, slot):
        return pltpu.make_async_remote_copy(
            src_ref=src, dst_ref=dst.at[slot], send_sem=send.at[k], recv_sem=recv.at[k],
            device_id=at(wrap(y + k), z, c), device_id_type=MESH)

    def f1(k):
        return ring_copy(fact_send.at[wrap(y + k)], fact_one, f1s, f1r, k, y)

    def f2(k):
        return pltpu.make_async_remote_copy(
            src_ref=fact_two_send, dst_ref=fact_two.at[z * 2 + c], send_sem=f2s.at[k], recv_sem=f2r.at[k],
            device_id=(me, y * group + peer(k)), device_id_type=MESH)

    def f3(k):
        return ring_copy(fact_three_send, fact_three, f3s, f3r, k, y)

    for k in range(1, ring):
        f1(k).start()
    fact_one[y] = fact_send[y]

    own.wait()
    for k in range(1, experts):
        mix(k).wait_recv()
    rows[y, z, c] = jnp.concatenate([mixed[e] for e in range(experts)], axis=0)

    def piece(yy, zz, far):
        return rows.at[yy, zz, c, :, pl.ds(0, along) if far else pl.ds(along, across)]

    def step(yy, zz, far, up, send, recv):
        ref = piece(yy, zz, far)
        return pltpu.make_async_remote_copy(
            src_ref=ref, dst_ref=ref, send_sem=send, recv_sem=recv,
            device_id=at(wrap(y + up), z, c), device_id_type=MESH)

    def far_step(hop, zz, long):
        up = sign if long else -sign
        yy = wrap(y - up * hop)
        send = (far_long if long else far_short).at[hop, zz]
        return step(yy, zz, True, up, send, far_recv.at[yy, zz])

    def near_step(hop, long):
        up = sign if long else -sign
        yy = wrap(y - up * hop)
        send = (near_long if long else near_short).at[hop]
        return step(yy, z, False, up, send, near_recv.at[yy, z])

    def far_arrive(hop, zz, long):
        up = sign if long else -sign
        yy = wrap(y - up * hop)
        step(yy, zz, True, up, far_long.at[0, 0], far_recv.at[yy, zz]).wait_recv()

    def near_arrive(hop, long):
        up = sign if long else -sign
        yy = wrap(y - up * hop)
        step(yy, z, False, up, near_long.at[0], near_recv.at[yy, z]).wait_recv()

    def run_step(yy, k, far):
        ref = piece(yy, z, far)
        return pltpu.make_async_remote_copy(
            src_ref=ref, dst_ref=ref, send_sem=run_far.at[k] if far else run_near.at[yy, k],
            recv_sem=(far_recv if far else near_recv).at[yy, z],
            device_id=at(y, lax.rem(z + k, run), c), device_id_type=MESH)

    def run_arrive(yy, k, far):
        zz = lax.rem(z + run - k, run)
        ref = piece(yy, zz, far)
        pltpu.make_async_remote_copy(
            src_ref=ref, dst_ref=ref, send_sem=run_far.at[k],
            recv_sem=(far_recv if far else near_recv).at[yy, zz],
            device_id=at(y, zz, c), device_id_type=MESH).wait_recv()

    def pair(yy, cc):
        ref = rows.at[yy, :, cc]
        return pltpu.make_async_remote_copy(
            src_ref=ref, dst_ref=ref, send_sem=pair_send.at[yy], recv_sem=pair_recv.at[yy],
            device_id=at(y, z, 1 - c), device_id_type=MESH)

    near_step(0, True).start()
    near_step(0, False).start()
    far_step(0, z, True).start()
    far_step(0, z, False).start()
    for k in range(1, run):
        run_step(y, k, True).start()
    for k in range(1, run):
        run_step(y, k, False).start()

    for k in range(1, ring):
        f1(k).wait_recv()
    fact_two_send[...] = functools.reduce(lambda a, b: a + b, [fact_one[i] for i in range(ring)])
    for k in range(1, group):
        f2(k).start()
    fact_two[z * 2 + c] = fact_two_send[...]

    def near_turn(hop):
        near_arrive(hop, True)
        if hop < half:
            near_step(hop, True).start()
            near_arrive(hop, False)
            if hop < half - 1:
                near_step(hop, False).start()

    def near_out(hop):
        for k in range(1, run):
            run_step(wrap(y - sign * hop), k, False).start()
        if hop < half:
            for k in range(1, run):
                run_step(wrap(y + sign * hop), k, False).start()

    def far_turn(hop, zz):
        far_arrive(hop, zz, True)
        pl.when(hop < half)(lambda: far_step(hop, zz, True).start())

        @pl.when(hop < half)
        def _():
            far_arrive(hop, zz, False)
            pl.when(hop < half - 1)(lambda: far_step(hop, zz, False).start())

    for hop in range(1, half + 1):
        near_turn(hop)
        far_turn(jnp.int32(hop), z)
        if hop == half // 2:
            for k in range(1, run):
                run_arrive(y, k, True)
                zz = lax.rem(z + run - k, run)
                far_step(0, zz, True).start()
                far_step(0, zz, False).start()
            for k in range(1, group):
                f2(k).wait_recv()
            fact_three_send[...] = functools.reduce(lambda a, b: a + b, [fact_two[i] for i in range(group)])
            for k in range(1, ring):
                f3(k).start()
            fact_three[y] = fact_three_send[...]
            for earlier in range(1, hop):
                near_out(earlier)
        if hop >= half // 2:
            near_out(hop)

    for k in range(1, run):
        run_arrive(y, k, False)
    pair(y, c).start()

    load_down.wait()
    left_out[0] = jnp.zeros(left_out.shape[1:], F32)

    def store(yy):
        return pltpu.make_async_copy(
            hidden.at[yy], hidden_hbm.at[0, pl.ds(pl.multiple_of(yy * batch, batch), batch), :], store_sem.at[yy])

    def compute(yy):
        pair(yy, 1 - c).wait_recv()
        factor = fact_three[yy].astype(BF16)
        units = down.shape[0]

        def body(i, carry):
            wide, low = carry
            columns = pl.ds(pl.multiple_of(i * chunk, chunk), chunk)
            x = rows[yy, :, :, :, columns].reshape(batch, chunk)
            wide = wide + lax.dot_general(x, down[:, columns], NT, preferred_element_type=F32)
            low = low + lax.dot_general(x, right_ref[0, :, columns], NT, preferred_element_type=F32)
            right_part[yy, :, columns] = jnp.dot(factor, x, preferred_element_type=F32)
            return wide, low

        wide, low = lax.fori_loop(
            0, width // chunk, body, (jnp.zeros((batch, units), F32), jnp.zeros((batch, rank), F32)))
        low = low.astype(BF16)
        delta = jnp.dot(low, left_ref[0], preferred_element_type=F32)
        hidden[yy] = (wide + 2.0 * delta).astype(BF16)
        store(yy).start()
        mine = state[pl.ds(pl.multiple_of(yy * batch, batch), batch), :]
        left_out[0] += 2.0 * lax.dot_general(low, mine, TN, preferred_element_type=F32)

    def order(n):
        hop = (n + 1) // 2
        return wrap(y + jnp.where(n % 2 == 1, -sign, sign) * hop)

    first = run // 2

    def turn(t, _):
        hop = t // 2 + 1

        @pl.when(t % 2 == 0)
        def _():
            for k in range(1, first):
                far_turn(hop, lax.rem(z + run - k, run))

        @pl.when(t % 2 == 1)
        def _():
            for k in range(first, run):
                far_turn(hop, lax.rem(z + run - k, run))
            yy = wrap(y - sign * hop)
            for k in range(1, run):
                run_arrive(yy, k, False)
            pair(yy, c).start()

            @pl.when(hop < half)
            def _():
                back = wrap(y + sign * hop)
                for k in range(1, run):
                    run_arrive(back, k, False)
                pair(back, c).start()

        @pl.when(t == 0)
        def _():
            for k in range(1, ring):
                f3(k).wait_recv()

        def one(n, _):
            compute(order(n))
            return 0

        start = jnp.where(t < 2 * half - 1, jnp.maximum(t - 1, 0), ring - 1)
        lax.fori_loop(start, jnp.where(t < 2 * half - 2, t, ring - 1), one, 0)
        return 0

    lax.fori_loop(0, 2 * half, turn, 0)
    compute(order(ring - 1))

    right_out[0] = 2.0 * functools.reduce(lambda a, b: a + b, [right_part[i] for i in range(ring)])

    for k in range(1, experts):
        mix(k).wait_send()
    for k in range(1, ring):
        f1(k).wait_send()
        f3(k).wait_send()
    for k in range(1, group):
        f2(k).wait_send()
    for k in range(1, run):
        run_step(y, k, True).wait_send()

    def drain(i, _):
        store(i).wait()
        pair(i, c).wait_send()
        for k in range(1, run):
            run_step(i, k, False).wait_send()
        return 0

    lax.fori_loop(0, ring, drain, 0)
    for hop in range(half):
        near_step(hop, True).wait_send()
        if hop < half - 1:
            near_step(hop, False).wait_send()
        for zz in range(run):
            far_step(hop, zz, True).wait_send()
            if hop < half - 1:
                far_step(hop, zz, False).wait_send()


def finish(a, b, c, a_out, b_out, c_out, a_mid, b_mid, c_mid, load, store):
    parts = [(a, a_mid, a_out), (b, b_mid, b_out), (c, c_mid, c_out)]
    loads = [pltpu.make_async_copy(x, m, load.at[i]) for i, (x, m, o) in enumerate(parts)]
    stores = [pltpu.make_async_copy(m, o, store.at[i]) for i, (x, m, o) in enumerate(parts)]
    for copy in loads:
        copy.start()
    for copy, after in zip(loads, stores):
        copy.wait()
        after.start()
    for copy in stores:
        copy.wait()


def shards(ring, run, across, chunk, limit, grad, gates, index, state, down, left, right):
    experts = lax.axis_size("expert")
    width = grad.shape[1]
    slots, units = state.shape[1:]
    rank = right.shape[1]
    half, group = ring // 2, run * 2
    block = slots // (ring * group)
    cap = block // experts
    batch = group * block
    dma = pltpu.SemaphoreType.DMA
    vmem = pl.BlockSpec(memory_space=pltpu.VMEM)
    smem = pl.BlockSpec(memory_space=pltpu.SMEM)
    hbm = pl.BlockSpec(memory_space=pl.ANY)
    results = pl.pallas_call(
        functools.partial(kernel, ring, run, across, chunk),
        out_shape=(
            jax.ShapeDtypeStruct((1, slots, units), BF16),
            jax.ShapeDtypeStruct((1, rank, units), F32),
            jax.ShapeDtypeStruct((1, rank, width), F32),
        ),
        in_specs=[vmem, smem, smem, hbm, hbm, vmem, vmem],
        out_specs=(hbm, vmem, vmem),
        scratch_shapes=[
            pltpu.VMEM((experts, cap, width), BF16),
            pltpu.VMEM((experts, cap, width), BF16),
            pltpu.VMEM((ring, run, 2, block, width), BF16),
            pltpu.VMEM((units, width), BF16),
            pltpu.VMEM((slots, units), BF16),
            pltpu.VMEM((ring, batch, units), BF16),
            pltpu.VMEM((ring, rank, width), F32),
            pltpu.VMEM((ring, rank, batch), F32),
            pltpu.VMEM((ring, rank, batch), F32),
            pltpu.VMEM((rank, batch), F32),
            pltpu.VMEM((group, rank, batch), F32),
            pltpu.VMEM((rank, batch), F32),
            pltpu.VMEM((ring, rank, batch), F32),
            dma((2,)), dma((ring,)), dma, dma((experts,)), dma((experts,)),
            dma((ring, run)), dma((ring, run)), dma((half, run)), dma((half, run)),
            dma((half,)), dma((half,)), dma((run,)), dma((ring, run)),
            dma((ring,)), dma((ring,)),
            dma((ring,)), dma((ring,)), dma((group,)), dma((group,)), dma((ring,)), dma((ring,)),
        ],
        compiler_params=pltpu.CompilerParams(
            collective_id=0, has_side_effects=True, vmem_limit_bytes=limit),
    )(grad, gates.T, index.T, state, down, jnp.swapaxes(left, 1, 2), right)
    hidden_gradient, left_gradient, right_gradient = pl.pallas_call(
        finish,
        out_shape=tuple(jax.ShapeDtypeStruct(r.shape, r.dtype) for r in results),
        in_specs=[hbm] * 3,
        out_specs=(hbm,) * 3,
        scratch_shapes=[pltpu.VMEM(r.shape, r.dtype) for r in results] + [dma((3,)), dma((3,))],
        compiler_params=pltpu.CompilerParams(vmem_limit_bytes=limit),
    )(*results)
    return hidden_gradient, jnp.swapaxes(left_gradient, 1, 2), right_gradient


def solution(mesh, **sizes):
    in_specs = (
        P(("expert", "dp"), None),
        P(("expert", "dp"), None),
        P(("expert", "dp"), None),
        P("expert", None, "dp"),
        P("expert", "dp", None),
        P("expert", "dp", None),
        P("expert", None, None),
    )
    out_specs = (P("expert", None, "dp"), P("expert", "dp", None), P("expert", None, None))
    sizes = dict(SIZES, **sizes)
    body = functools.partial(
        shards, sizes["ring"], sizes["run"], sizes["across"], sizes["chunk"], sizes["limit"])
    return jax.shard_map(body, mesh=mesh, in_specs=in_specs, out_specs=out_specs, check_vma=False)
```

```python
import functools

import jax
import jax.numpy as jnp
from jax import lax
from jax.experimental import pallas as pl
from jax.experimental.pallas import tpu as pltpu
from jax.sharding import PartitionSpec as P

MESH = pl.DeviceIdType.MESH
F32, BF16 = jnp.float32, jnp.bfloat16
NT = (((1,), (1,)), ((), ()))
TN = (((0,), (0,)), ((), ()))

SIZES = dict(ring=8, run=4, across=1536, chunk=3072, limit=60 * 2**20)


def kernel(
    ring, run, across, chunk,
    grad_ref, gates_ref, index_ref, state_hbm, down_hbm, left_ref, right_ref,
    hidden_hbm, left_out, right_out,
    slots, mixed, rows, down, state, hidden, right_part,
    fact_send, fact_one, fact_two_send, fact_two, fact_three_send, fact_three,
    load_sem, store_sem, own_sem, mix_send, mix_recv,
    far_recv, near_recv, far_long, far_short, near_long, near_short, run_far, run_near,
    pair_send, pair_recv, f1s, f1r, f2s, f2r, f3s, f3r,
):
    width = grad_ref.shape[1]
    top, tokens = gates_ref.shape
    experts = slots.shape[0]
    cap = slots.shape[1]
    half = ring // 2
    group = run * 2
    block = experts * cap
    batch = group * block
    rank = left_ref.shape[1]
    along = width - across
    me = lax.axis_index("expert")
    v = lax.axis_index("dp")
    y, z, c = v // group, (v // 2) % run, v % 2
    sign = 1 - 2 * c

    def at(yy, zz, cc):
        return (me, (yy * run + zz) * 2 + cc)

    def wrap(value):
        return lax.rem(value + 2 * ring, ring)

    def peer(k):
        return lax.rem(z * 2 + c + k, group)

    load_down = pltpu.make_async_copy(down_hbm.at[0], down, load_sem.at[0])
    load_state = pltpu.make_async_copy(state_hbm.at[0], state, load_sem.at[1])
    load_state.start()
    load_down.start()

    barrier = pltpu.get_barrier_semaphore()
    for k in range(1, experts):
        pl.semaphore_signal(barrier, 1, device_id=(lax.rem(me + k, experts), v), device_id_type=MESH)
    for k in range(1, ring):
        pl.semaphore_signal(barrier, 1, device_id=at(wrap(y + k), z, c), device_id_type=MESH)
    for k in range(1, group):
        pl.semaphore_signal(barrier, 1, device_id=(me, y * group + peer(k)), device_id_type=MESH)

    chosen = [[index_ref[k, t] for k in range(top)] for t in range(tokens)]
    flat = [chosen[t][k] for t in range(tokens) for k in range(top)]
    place = lax.broadcasted_iota(jnp.int32, (block, 1), 0)
    total = jnp.zeros((block, width), F32)
    for t in range(tokens):
        weight = jnp.zeros((block, 1), F32)
        for k in range(top):
            position = jnp.int32(0)
            for earlier in flat[: t * top + k]:
                position = position + (earlier == chosen[t][k]).astype(jnp.int32)
            slot = chosen[t][k] * cap + position
            weight = weight + jnp.where(place == slot, gates_ref[k, t], jnp.float32(0))
        total = total + weight * grad_ref[pl.ds(t, 1), :].astype(F32)
    total = total.astype(BF16)
    for e in range(experts):
        slots[e] = total[e * cap:(e + 1) * cap, :]

    pl.semaphore_wait(barrier, experts + ring + group - 3)

    def mix(k):
        other = lax.rem(me + k, experts)
        return pltpu.make_async_remote_copy(
            src_ref=slots.at[other], dst_ref=mixed.at[me], send_sem=mix_send.at[k],
            recv_sem=mix_recv.at[k], device_id=(other, v), device_id_type=MESH)

    for k in range(1, experts):
        mix(k).start()
    own = pltpu.make_async_copy(slots.at[me], mixed.at[me], own_sem)
    own.start()

    load_state.wait()
    part = lax.dot_general(left_ref[0], state[...], NT, preferred_element_type=F32)
    for i in range(ring):
        fact_send[i] = part[:, i * batch:(i + 1) * batch]

    def ring_copy(src, dst, send, recv, k, slot):
        return pltpu.make_async_remote_copy(
            src_ref=src, dst_ref=dst.at[slot], send_sem=send.at[k], recv_sem=recv.at[k],
            device_id=at(wrap(y + k), z, c), device_id_type=MESH)

    def f1(k):
        return ring_copy(fact_send.at[wrap(y + k)], fact_one, f1s, f1r, k, y)

    def f2(k):
        return pltpu.make_async_remote_copy(
            src_ref=fact_two_send, dst_ref=fact_two.at[z * 2 + c], send_sem=f2s.at[k], recv_sem=f2r.at[k],
            device_id=(me, y * group + peer(k)), device_id_type=MESH)

    def f3(k):
        return ring_copy(fact_three_send, fact_three, f3s, f3r, k, y)

    for k in range(1, ring):
        f1(k).start()
    fact_one[y] = fact_send[y]

    own.wait()
    for k in range(1, experts):
        mix(k).wait_recv()
    rows[y, z, c] = jnp.concatenate([mixed[e] for e in range(experts)], axis=0)

    def piece(yy, zz, far):
        return rows.at[yy, zz, c, :, pl.ds(0, along) if far else pl.ds(along, across)]

    def step(yy, zz, far, up, send, recv):
        ref = piece(yy, zz, far)
        return pltpu.make_async_remote_copy(
            src_ref=ref, dst_ref=ref, send_sem=send, recv_sem=recv,
            device_id=at(wrap(y + up), z, c), device_id_type=MESH)

    def far_step(hop, zz, long):
        up = sign if long else -sign
        yy = wrap(y - up * hop)
        send = (far_long if long else far_short).at[hop, zz]
        return step(yy, zz, True, up, send, far_recv.at[yy, zz])

    def near_step(hop, long):
        up = sign if long else -sign
        yy = wrap(y - up * hop)
        send = (near_long if long else near_short).at[hop]
        return step(yy, z, False, up, send, near_recv.at[yy, z])

    def far_arrive(hop, zz, long):
        up = sign if long else -sign
        yy = wrap(y - up * hop)
        step(yy, zz, True, up, far_long.at[0, 0], far_recv.at[yy, zz]).wait_recv()

    def near_arrive(hop, long):
        up = sign if long else -sign
        yy = wrap(y - up * hop)
        step(yy, z, False, up, near_long.at[0], near_recv.at[yy, z]).wait_recv()

    def run_step(yy, k, far):
        ref = piece(yy, z, far)
        return pltpu.make_async_remote_copy(
            src_ref=ref, dst_ref=ref, send_sem=run_far.at[k] if far else run_near.at[yy, k],
            recv_sem=(far_recv if far else near_recv).at[yy, z],
            device_id=at(y, lax.rem(z + k, run), c), device_id_type=MESH)

    def run_arrive(yy, k, far):
        zz = lax.rem(z + run - k, run)
        ref = piece(yy, zz, far)
        pltpu.make_async_remote_copy(
            src_ref=ref, dst_ref=ref, send_sem=run_far.at[k],
            recv_sem=(far_recv if far else near_recv).at[yy, zz],
            device_id=at(y, zz, c), device_id_type=MESH).wait_recv()

    def pair(yy, cc):
        ref = rows.at[yy, :, cc]
        return pltpu.make_async_remote_copy(
            src_ref=ref, dst_ref=ref, send_sem=pair_send.at[yy], recv_sem=pair_recv.at[yy],
            device_id=at(y, z, 1 - c), device_id_type=MESH)

    near_step(0, True).start()
    near_step(0, False).start()
    far_step(0, z, True).start()
    far_step(0, z, False).start()
    for k in range(1, run):
        run_step(y, k, True).start()
    for k in range(1, run):
        run_step(y, k, False).start()

    for k in range(1, ring):
        f1(k).wait_recv()
    fact_two_send[...] = functools.reduce(lambda a, b: a + b, [fact_one[i] for i in range(ring)])
    for k in range(1, group):
        f2(k).start()
    fact_two[z * 2 + c] = fact_two_send[...]

    def near_turn(hop):
        near_arrive(hop, True)
        if hop < half:
            near_step(hop, True).start()
            near_arrive(hop, False)
            if hop < half - 1:
                near_step(hop, False).start()

    def near_out(hop):
        for k in range(1, run):
            run_step(wrap(y - sign * hop), k, False).start()
        if hop < half:
            for k in range(1, run):
                run_step(wrap(y + sign * hop), k, False).start()

    def far_turn(hop, zz):
        far_arrive(hop, zz, True)
        pl.when(hop < half)(lambda: far_step(hop, zz, True).start())

        @pl.when(hop < half)
        def _():
            far_arrive(hop, zz, False)
            pl.when(hop < half - 1)(lambda: far_step(hop, zz, False).start())

    for hop in range(1, half + 1):
        near_turn(hop)
        far_turn(jnp.int32(hop), z)
        if hop == half // 2:
            for k in range(1, run):
                run_arrive(y, k, True)
                zz = lax.rem(z + run - k, run)
                far_step(0, zz, True).start()
                far_step(0, zz, False).start()
            for k in range(1, group):
                f2(k).wait_recv()
            fact_three_send[...] = functools.reduce(lambda a, b: a + b, [fact_two[i] for i in range(group)])
            for k in range(1, ring):
                f3(k).start()
            fact_three[y] = fact_three_send[...]
            for earlier in range(1, hop):
                near_out(earlier)
        if hop >= half // 2:
            near_out(hop)

    for k in range(1, run):
        run_arrive(y, k, False)
    pair(y, c).start()

    load_down.wait()
    left_out[0] = jnp.zeros(left_out.shape[1:], F32)

    def store(yy):
        return pltpu.make_async_copy(
            hidden.at[yy], hidden_hbm.at[0, pl.ds(pl.multiple_of(yy * batch, batch), batch), :], store_sem.at[yy])

    def compute(yy):
        pair(yy, 1 - c).wait_recv()
        factor = fact_three[yy].astype(BF16)
        units = down.shape[0]

        def body(i, carry):
            wide, low = carry
            columns = pl.ds(pl.multiple_of(i * chunk, chunk), chunk)
            x = rows[yy, :, :, :, columns].reshape(batch, chunk)
            wide = wide + lax.dot_general(x, down[:, columns], NT, preferred_element_type=F32)
            low = low + lax.dot_general(x, right_ref[0, :, columns], NT, preferred_element_type=F32)
            right_part[yy, :, columns] = jnp.dot(factor, x, preferred_element_type=F32)
            return wide, low

        wide, low = lax.fori_loop(
            0, width // chunk, body, (jnp.zeros((batch, units), F32), jnp.zeros((batch, rank), F32)))
        low = low.astype(BF16)
        delta = jnp.dot(low, left_ref[0], preferred_element_type=F32)
        hidden[yy] = (wide + 2.0 * delta).astype(BF16)
        store(yy).start()
        mine = state[pl.ds(pl.multiple_of(yy * batch, batch), batch), :]
        left_out[0] += 2.0 * lax.dot_general(low, mine, TN, preferred_element_type=F32)

    def order(n):
        hop = (n + 1) // 2
        return wrap(y + jnp.where(n % 2 == 1, -sign, sign) * hop)

    first = run // 2

    def turn(t, _):
        hop = t // 2 + 1

        @pl.when(t % 2 == 0)
        def _():
            for k in range(1, first):
                far_turn(hop, lax.rem(z + run - k, run))

        @pl.when(t % 2 == 1)
        def _():
            for k in range(first, run):
                far_turn(hop, lax.rem(z + run - k, run))
            yy = wrap(y - sign * hop)
            for k in range(1, run):
                run_arrive(yy, k, False)
            pair(yy, c).start()

            @pl.when(hop < half)
            def _():
                back = wrap(y + sign * hop)
                for k in range(1, run):
                    run_arrive(back, k, False)
                pair(back, c).start()

        @pl.when(t == 0)
        def _():
            for k in range(1, ring):
                f3(k).wait_recv()

        def one(n, _):
            compute(order(n))
            return 0

        start = jnp.where(t < 2 * half - 1, jnp.maximum(t - 1, 0), ring - 1)
        lax.fori_loop(start, jnp.where(t < 2 * half - 2, t, ring - 1), one, 0)
        return 0

    lax.fori_loop(0, 2 * half, turn, 0)
    for k in range(1, experts):
        mix(k).wait_send()
    for k in range(1, ring):
        f1(k).wait_send()
        f3(k).wait_send()
    for k in range(1, group):
        f2(k).wait_send()
    for k in range(1, run):
        run_step(y, k, True).wait_send()

    def drain(i, _):
        for k in range(1, run):
            run_step(i, k, False).wait_send()
        return 0

    lax.fori_loop(0, ring, drain, 0)
    for hop in range(half):
        near_step(hop, True).wait_send()
        if hop < half - 1:
            near_step(hop, False).wait_send()
        for zz in range(run):
            far_step(hop, zz, True).wait_send()
            if hop < half - 1:
                far_step(hop, zz, False).wait_send()

    compute(order(ring - 1))

    right_out[0] = 2.0 * functools.reduce(lambda a, b: a + b, [right_part[i] for i in range(ring)])

    def finished(i, _):
        store(i).wait()
        pair(i, c).wait_send()
        return 0

    lax.fori_loop(0, ring, finished, 0)


def finish(a, b, c, a_out, b_out, c_out, a_mid, b_mid, c_mid, load, store):
    parts = [(a, a_mid, a_out), (b, b_mid, b_out), (c, c_mid, c_out)]
    loads = [pltpu.make_async_copy(x, m, load.at[i]) for i, (x, m, o) in enumerate(parts)]
    stores = [pltpu.make_async_copy(m, o, store.at[i]) for i, (x, m, o) in enumerate(parts)]
    for copy in loads:
        copy.start()
    for copy, after in zip(loads, stores):
        copy.wait()
        after.start()
    for copy in stores:
        copy.wait()


def shards(ring, run, across, chunk, limit, grad, gates, index, state, down, left, right):
    experts = lax.axis_size("expert")
    width = grad.shape[1]
    slots, units = state.shape[1:]
    rank = right.shape[1]
    half, group = ring // 2, run * 2
    block = slots // (ring * group)
    cap = block // experts
    batch = group * block
    dma = pltpu.SemaphoreType.DMA
    vmem = pl.BlockSpec(memory_space=pltpu.VMEM)
    smem = pl.BlockSpec(memory_space=pltpu.SMEM)
    hbm = pl.BlockSpec(memory_space=pl.ANY)
    results = pl.pallas_call(
        functools.partial(kernel, ring, run, across, chunk),
        out_shape=(
            jax.ShapeDtypeStruct((1, slots, units), BF16),
            jax.ShapeDtypeStruct((1, rank, units), F32),
            jax.ShapeDtypeStruct((1, rank, width), F32),
        ),
        in_specs=[vmem, smem, smem, hbm, hbm, vmem, vmem],
        out_specs=(hbm, vmem, vmem),
        scratch_shapes=[
            pltpu.VMEM((experts, cap, width), BF16),
            pltpu.VMEM((experts, cap, width), BF16),
            pltpu.VMEM((ring, run, 2, block, width), BF16),
            pltpu.VMEM((units, width), BF16),
            pltpu.VMEM((slots, units), BF16),
            pltpu.VMEM((ring, batch, units), BF16),
            pltpu.VMEM((ring, rank, width), F32),
            pltpu.VMEM((ring, rank, batch), F32),
            pltpu.VMEM((ring, rank, batch), F32),
            pltpu.VMEM((rank, batch), F32),
            pltpu.VMEM((group, rank, batch), F32),
            pltpu.VMEM((rank, batch), F32),
            pltpu.VMEM((ring, rank, batch), F32),
            dma((2,)), dma((ring,)), dma, dma((experts,)), dma((experts,)),
            dma((ring, run)), dma((ring, run)), dma((half, run)), dma((half, run)),
            dma((half,)), dma((half,)), dma((run,)), dma((ring, run)),
            dma((ring,)), dma((ring,)),
            dma((ring,)), dma((ring,)), dma((group,)), dma((group,)), dma((ring,)), dma((ring,)),
        ],
        compiler_params=pltpu.CompilerParams(
            collective_id=0, has_side_effects=True, vmem_limit_bytes=limit),
    )(grad, gates.T, index.T, state, down, jnp.swapaxes(left, 1, 2), right)
    hidden_gradient, left_gradient, right_gradient = pl.pallas_call(
        finish,
        out_shape=tuple(jax.ShapeDtypeStruct(r.shape, r.dtype) for r in results),
        in_specs=[hbm] * 3,
        out_specs=(hbm,) * 3,
        scratch_shapes=[pltpu.VMEM(r.shape, r.dtype) for r in results] + [dma((3,)), dma((3,))],
        compiler_params=pltpu.CompilerParams(vmem_limit_bytes=limit),
    )(*results)
    return hidden_gradient, jnp.swapaxes(left_gradient, 1, 2), right_gradient


def solution(mesh, **sizes):
    in_specs = (
        P(("expert", "dp"), None),
        P(("expert", "dp"), None),
        P(("expert", "dp"), None),
        P("expert", None, "dp"),
        P("expert", "dp", None),
        P("expert", "dp", None),
        P("expert", None, None),
    )
    out_specs = (P("expert", None, "dp"), P("expert", "dp", None), P("expert", None, None))
    sizes = dict(SIZES, **sizes)
    body = functools.partial(
        shards, sizes["ring"], sizes["run"], sizes["across"], sizes["chunk"], sizes["limit"])
    return jax.shard_map(body, mesh=mesh, in_specs=in_specs, out_specs=out_specs, check_vma=False)
```

```python
import functools

import jax
import jax.numpy as jnp
from jax import lax
from jax.experimental import pallas as pl
from jax.experimental.pallas import tpu as pltpu
from jax.sharding import PartitionSpec as P

MESH = pl.DeviceIdType.MESH
F32, BF16 = jnp.float32, jnp.bfloat16
NT = (((1,), (1,)), ((), ()))
TN = (((0,), (0,)), ((), ()))

SIZES = dict(ring=8, run=4, across=1536, chunk=3072, limit=60 * 2**20)


def kernel(
    ring, run, across, chunk,
    grad_hbm, gates_ref, index_ref, state_hbm, down_hbm, left_hbm, right_hbm,
    hidden_hbm, left_out, right_out,
    grad_ref, left_ref, right_ref, slots, mixed, rows, down, state, hidden, right_part,
    fact_send, fact_one, fact_two_send, fact_two, fact_three_send, fact_three,
    load_sem, store_sem, own_sem, mix_send, mix_recv,
    far_recv, near_recv, far_long, far_short, near_long, near_short, run_far, run_near,
    pair_send, pair_recv, f1s, f1r, f2s, f2r, f3s, f3r,
):
    width = grad_ref.shape[1]
    top, tokens = gates_ref.shape
    experts = slots.shape[0]
    cap = slots.shape[1]
    half = ring // 2
    group = run * 2
    block = experts * cap
    batch = group * block
    rank = left_ref.shape[1]
    along = width - across
    me = lax.axis_index("expert")
    v = lax.axis_index("dp")
    y, z, c = v // group, (v // 2) % run, v % 2
    sign = 1 - 2 * c

    def at(yy, zz, cc):
        return (me, (yy * run + zz) * 2 + cc)

    def wrap(value):
        return lax.rem(value + 2 * ring, ring)

    def peer(k):
        return lax.rem(z * 2 + c + k, group)

    load_down = pltpu.make_async_copy(down_hbm.at[0], down, load_sem.at[0])
    load_state = pltpu.make_async_copy(state_hbm.at[0], state, load_sem.at[1])

    barrier = pltpu.get_barrier_semaphore()
    for k in range(1, experts):
        pl.semaphore_signal(barrier, 1, device_id=(lax.rem(me + k, experts), v), device_id_type=MESH)
    for k in range(1, ring):
        pl.semaphore_signal(barrier, 1, device_id=at(wrap(y + k), z, c), device_id_type=MESH)
    for k in range(1, group):
        pl.semaphore_signal(barrier, 1, device_id=(me, y * group + peer(k)), device_id_type=MESH)

    loads = [
        pltpu.make_async_copy(src, dst, load_sem.at[2 + i])
        for i, (src, dst) in enumerate([(grad_hbm, grad_ref), (left_hbm, left_ref), (right_hbm, right_ref)])
    ]
    for load in loads:
        load.start()
    load_state.start()
    load_down.start()
    loads[0].wait()

    chosen = [[index_ref[k, t] for k in range(top)] for t in range(tokens)]
    flat = [chosen[t][k] for t in range(tokens) for k in range(top)]
    place = lax.broadcasted_iota(jnp.int32, (block, 1), 0)
    total = jnp.zeros((block, width), F32)
    for t in range(tokens):
        weight = jnp.zeros((block, 1), F32)
        for k in range(top):
            position = jnp.int32(0)
            for earlier in flat[: t * top + k]:
                position = position + (earlier == chosen[t][k]).astype(jnp.int32)
            slot = chosen[t][k] * cap + position
            weight = weight + jnp.where(place == slot, gates_ref[k, t], jnp.float32(0))
        total = total + weight * grad_ref[pl.ds(t, 1), :].astype(F32)
    total = total.astype(BF16)
    for e in range(experts):
        slots[e] = total[e * cap:(e + 1) * cap, :]

    pl.semaphore_wait(barrier, experts + ring + group - 3)

    def mix(k):
        other = lax.rem(me + k, experts)
        return pltpu.make_async_remote_copy(
            src_ref=slots.at[other], dst_ref=mixed.at[me], send_sem=mix_send.at[k],
            recv_sem=mix_recv.at[k], device_id=(other, v), device_id_type=MESH)

    for k in range(1, experts):
        mix(k).start()
    own = pltpu.make_async_copy(slots.at[me], mixed.at[me], own_sem)
    own.start()

    load_state.wait()
    loads[1].wait()
    loads[2].wait()
    part = lax.dot_general(left_ref[0], state[...], NT, preferred_element_type=F32)
    for i in range(ring):
        fact_send[i] = part[:, i * batch:(i + 1) * batch]

    def ring_copy(src, dst, send, recv, k, slot):
        return pltpu.make_async_remote_copy(
            src_ref=src, dst_ref=dst.at[slot], send_sem=send.at[k], recv_sem=recv.at[k],
            device_id=at(wrap(y + k), z, c), device_id_type=MESH)

    def f1(k):
        return ring_copy(fact_send.at[wrap(y + k)], fact_one, f1s, f1r, k, y)

    def f2(k):
        return pltpu.make_async_remote_copy(
            src_ref=fact_two_send, dst_ref=fact_two.at[z * 2 + c], send_sem=f2s.at[k], recv_sem=f2r.at[k],
            device_id=(me, y * group + peer(k)), device_id_type=MESH)

    def f3(k):
        return ring_copy(fact_three_send, fact_three, f3s, f3r, k, y)

    for k in range(1, ring):
        f1(k).start()
    fact_one[y] = fact_send[y]

    own.wait()
    for k in range(1, experts):
        mix(k).wait_recv()
    rows[y, z, c] = jnp.concatenate([mixed[e] for e in range(experts)], axis=0)

    def piece(yy, zz, far):
        return rows.at[yy, zz, c, :, pl.ds(0, along) if far else pl.ds(along, across)]

    def step(yy, zz, far, up, send, recv):
        ref = piece(yy, zz, far)
        return pltpu.make_async_remote_copy(
            src_ref=ref, dst_ref=ref, send_sem=send, recv_sem=recv,
            device_id=at(wrap(y + up), z, c), device_id_type=MESH)

    def far_step(hop, zz, long):
        up = sign if long else -sign
        yy = wrap(y - up * hop)
        send = (far_long if long else far_short).at[hop, zz]
        return step(yy, zz, True, up, send, far_recv.at[yy, zz])

    def near_step(hop, long):
        up = sign if long else -sign
        yy = wrap(y - up * hop)
        send = (near_long if long else near_short).at[hop]
        return step(yy, z, False, up, send, near_recv.at[yy, z])

    def far_arrive(hop, zz, long):
        up = sign if long else -sign
        yy = wrap(y - up * hop)
        step(yy, zz, True, up, far_long.at[0, 0], far_recv.at[yy, zz]).wait_recv()

    def near_arrive(hop, long):
        up = sign if long else -sign
        yy = wrap(y - up * hop)
        step(yy, z, False, up, near_long.at[0], near_recv.at[yy, z]).wait_recv()

    def run_step(yy, k, far):
        ref = piece(yy, z, far)
        return pltpu.make_async_remote_copy(
            src_ref=ref, dst_ref=ref, send_sem=run_far.at[k] if far else run_near.at[yy, k],
            recv_sem=(far_recv if far else near_recv).at[yy, z],
            device_id=at(y, lax.rem(z + k, run), c), device_id_type=MESH)

    def run_arrive(yy, k, far):
        zz = lax.rem(z + run - k, run)
        ref = piece(yy, zz, far)
        pltpu.make_async_remote_copy(
            src_ref=ref, dst_ref=ref, send_sem=run_far.at[k],
            recv_sem=(far_recv if far else near_recv).at[yy, zz],
            device_id=at(y, zz, c), device_id_type=MESH).wait_recv()

    def pair(yy, cc):
        ref = rows.at[yy, :, cc]
        return pltpu.make_async_remote_copy(
            src_ref=ref, dst_ref=ref, send_sem=pair_send.at[yy], recv_sem=pair_recv.at[yy],
            device_id=at(y, z, 1 - c), device_id_type=MESH)

    near_step(0, True).start()
    near_step(0, False).start()
    far_step(0, z, True).start()
    far_step(0, z, False).start()
    for k in range(1, run):
        run_step(y, k, True).start()
    for k in range(1, run):
        run_step(y, k, False).start()

    for k in range(1, ring):
        f1(k).wait_recv()
    fact_two_send[...] = functools.reduce(lambda a, b: a + b, [fact_one[i] for i in range(ring)])
    for k in range(1, group):
        f2(k).start()
    fact_two[z * 2 + c] = fact_two_send[...]

    def near_turn(hop):
        near_arrive(hop, True)
        if hop < half:
            near_step(hop, True).start()
            near_arrive(hop, False)
            if hop < half - 1:
                near_step(hop, False).start()

    def near_out(hop):
        for k in range(1, run):
            run_step(wrap(y - sign * hop), k, False).start()
        if hop < half:
            for k in range(1, run):
                run_step(wrap(y + sign * hop), k, False).start()

    def far_turn(hop, zz):
        far_arrive(hop, zz, True)
        pl.when(hop < half)(lambda: far_step(hop, zz, True).start())

        @pl.when(hop < half)
        def _():
            far_arrive(hop, zz, False)
            pl.when(hop < half - 1)(lambda: far_step(hop, zz, False).start())

    for hop in range(1, half + 1):
        near_turn(hop)
        far_turn(jnp.int32(hop), z)
        if hop == half // 2:
            for k in range(1, run):
                run_arrive(y, k, True)
                zz = lax.rem(z + run - k, run)
                far_step(0, zz, True).start()
                far_step(0, zz, False).start()
            for k in range(1, group):
                f2(k).wait_recv()
            fact_three_send[...] = functools.reduce(lambda a, b: a + b, [fact_two[i] for i in range(group)])
            for k in range(1, ring):
                f3(k).start()
            fact_three[y] = fact_three_send[...]
            for earlier in range(1, hop):
                near_out(earlier)
        if hop >= half // 2:
            near_out(hop)

    for k in range(1, run):
        run_arrive(y, k, False)
    pair(y, c).start()

    load_down.wait()
    left_out[0] = jnp.zeros(left_out.shape[1:], F32)

    def store(yy):
        return pltpu.make_async_copy(
            hidden.at[yy], hidden_hbm.at[0, pl.ds(pl.multiple_of(yy * batch, batch), batch), :], store_sem.at[yy])

    def compute(yy):
        pair(yy, 1 - c).wait_recv()
        factor = fact_three[yy].astype(BF16)
        units = down.shape[0]

        def body(i, carry):
            wide, low = carry
            columns = pl.ds(pl.multiple_of(i * chunk, chunk), chunk)
            x = rows[yy, :, :, :, columns].reshape(batch, chunk)
            wide = wide + lax.dot_general(x, down[:, columns], NT, preferred_element_type=F32)
            low = low + lax.dot_general(x, right_ref[0, :, columns], NT, preferred_element_type=F32)
            right_part[yy, :, columns] = jnp.dot(factor, x, preferred_element_type=F32)
            return wide, low

        wide, low = lax.fori_loop(
            0, width // chunk, body, (jnp.zeros((batch, units), F32), jnp.zeros((batch, rank), F32)))
        low = low.astype(BF16)
        delta = jnp.dot(low, left_ref[0], preferred_element_type=F32)
        hidden[yy] = (wide + 2.0 * delta).astype(BF16)
        store(yy).start()
        mine = state[pl.ds(pl.multiple_of(yy * batch, batch), batch), :]
        left_out[0] += 2.0 * lax.dot_general(low, mine, TN, preferred_element_type=F32)

    def order(n):
        hop = (n + 1) // 2
        return wrap(y + jnp.where(n % 2 == 1, -sign, sign) * hop)

    first = run // 2

    def turn(t, _):
        hop = t // 2 + 1

        @pl.when(t % 2 == 0)
        def _():
            for k in range(1, first):
                far_turn(hop, lax.rem(z + run - k, run))

        @pl.when(t % 2 == 1)
        def _():
            for k in range(first, run):
                far_turn(hop, lax.rem(z + run - k, run))
            yy = wrap(y - sign * hop)
            for k in range(1, run):
                run_arrive(yy, k, False)
            pair(yy, c).start()

            @pl.when(hop < half)
            def _():
                back = wrap(y + sign * hop)
                for k in range(1, run):
                    run_arrive(back, k, False)
                pair(back, c).start()

        @pl.when(t == 0)
        def _():
            for k in range(1, ring):
                f3(k).wait_recv()

        def one(n, _):
            compute(order(n))
            return 0

        start = jnp.where(t < 2 * half - 1, jnp.maximum(t - 1, 0), ring - 1)
        lax.fori_loop(start, jnp.where(t < 2 * half - 2, t, ring - 1), one, 0)
        return 0

    lax.fori_loop(0, 2 * half, turn, 0)
    compute(order(ring - 1))

    right_out[0] = 2.0 * functools.reduce(lambda a, b: a + b, [right_part[i] for i in range(ring)])

    for k in range(1, experts):
        mix(k).wait_send()
    for k in range(1, ring):
        f1(k).wait_send()
        f3(k).wait_send()
    for k in range(1, group):
        f2(k).wait_send()
    for k in range(1, run):
        run_step(y, k, True).wait_send()

    def drain(i, _):
        store(i).wait()
        pair(i, c).wait_send()
        for k in range(1, run):
            run_step(i, k, False).wait_send()
        return 0

    lax.fori_loop(0, ring, drain, 0)
    for hop in range(half):
        near_step(hop, True).wait_send()
        if hop < half - 1:
            near_step(hop, False).wait_send()
        for zz in range(run):
            far_step(hop, zz, True).wait_send()
            if hop < half - 1:
                far_step(hop, zz, False).wait_send()


def finish(a, b, c, a_out, b_out, c_out, a_mid, b_mid, c_mid, load, store):
    parts = [(a, a_mid, a_out), (b, b_mid, b_out), (c, c_mid, c_out)]
    loads = [pltpu.make_async_copy(x, m, load.at[i]) for i, (x, m, o) in enumerate(parts)]
    stores = [pltpu.make_async_copy(m, o, store.at[i]) for i, (x, m, o) in enumerate(parts)]
    for copy in loads:
        copy.start()
    for copy, after in zip(loads, stores):
        copy.wait()
        after.start()
    for copy in stores:
        copy.wait()


def shards(ring, run, across, chunk, limit, grad, gates, index, state, down, left, right):
    experts = lax.axis_size("expert")
    width = grad.shape[1]
    slots, units = state.shape[1:]
    rank = right.shape[1]
    half, group = ring // 2, run * 2
    block = slots // (ring * group)
    cap = block // experts
    batch = group * block
    dma = pltpu.SemaphoreType.DMA
    vmem = pl.BlockSpec(memory_space=pltpu.VMEM)
    smem = pl.BlockSpec(memory_space=pltpu.SMEM)
    hbm = pl.BlockSpec(memory_space=pl.ANY)
    results = pl.pallas_call(
        functools.partial(kernel, ring, run, across, chunk),
        out_shape=(
            jax.ShapeDtypeStruct((1, slots, units), BF16),
            jax.ShapeDtypeStruct((1, rank, units), F32),
            jax.ShapeDtypeStruct((1, rank, width), F32),
        ),
        in_specs=[hbm, smem, smem, hbm, hbm, hbm, hbm],
        out_specs=(hbm, vmem, vmem),
        scratch_shapes=[
            pltpu.VMEM(grad.shape, BF16),
            pltpu.VMEM((1, rank, units), BF16),
            pltpu.VMEM(right.shape, BF16),
            pltpu.VMEM((experts, cap, width), BF16),
            pltpu.VMEM((experts, cap, width), BF16),
            pltpu.VMEM((ring, run, 2, block, width), BF16),
            pltpu.VMEM((units, width), BF16),
            pltpu.VMEM((slots, units), BF16),
            pltpu.VMEM((ring, batch, units), BF16),
            pltpu.VMEM((ring, rank, width), F32),
            pltpu.VMEM((ring, rank, batch), F32),
            pltpu.VMEM((ring, rank, batch), F32),
            pltpu.VMEM((rank, batch), F32),
            pltpu.VMEM((group, rank, batch), F32),
            pltpu.VMEM((rank, batch), F32),
            pltpu.VMEM((ring, rank, batch), F32),
            dma((5,)), dma((ring,)), dma, dma((experts,)), dma((experts,)),
            dma((ring, run)), dma((ring, run)), dma((half, run)), dma((half, run)),
            dma((half,)), dma((half,)), dma((run,)), dma((ring, run)),
            dma((ring,)), dma((ring,)),
            dma((ring,)), dma((ring,)), dma((group,)), dma((group,)), dma((ring,)), dma((ring,)),
        ],
        compiler_params=pltpu.CompilerParams(
            collective_id=0, has_side_effects=True, vmem_limit_bytes=limit),
    )(grad, gates.T, index.T, state, down, jnp.swapaxes(left, 1, 2), right)
    hidden_gradient, left_gradient, right_gradient = pl.pallas_call(
        finish,
        out_shape=tuple(jax.ShapeDtypeStruct(r.shape, r.dtype) for r in results),
        in_specs=[hbm] * 3,
        out_specs=(hbm,) * 3,
        scratch_shapes=[pltpu.VMEM(r.shape, r.dtype) for r in results] + [dma((3,)), dma((3,))],
        compiler_params=pltpu.CompilerParams(vmem_limit_bytes=limit),
    )(*results)
    return hidden_gradient, jnp.swapaxes(left_gradient, 1, 2), right_gradient


def solution(mesh, **sizes):
    in_specs = (
        P(("expert", "dp"), None),
        P(("expert", "dp"), None),
        P(("expert", "dp"), None),
        P("expert", None, "dp"),
        P("expert", "dp", None),
        P("expert", "dp", None),
        P("expert", None, None),
    )
    out_specs = (P("expert", None, "dp"), P("expert", "dp", None), P("expert", None, None))
    sizes = dict(SIZES, **sizes)
    body = functools.partial(
        shards, sizes["ring"], sizes["run"], sizes["across"], sizes["chunk"], sizes["limit"])
    return jax.shard_map(body, mesh=mesh, in_specs=in_specs, out_specs=out_specs, check_vma=False)
```
